32 devices in a mesh: groups: 2 (over y), sec: 4 (over z), blk: 4 (over x, core).
Axes of the slice: x: 2, y: 2, z: 4, core: 2. Of those that a mesh axis runs over, the one named last changes fastest.
Arguments:
- psi: bfloat16 [8, 4, 256, 256], P(('groups', 'sec'), 'blk'), parts along dimension 0, may hold values from -6 to 6
- own_env: bfloat16 [8, 4, 17, 256, 256], P(('groups', 'sec'), 'blk'), parts along dimension 0, may hold values from -0.375 to 0.375
- handoff_env: bfloat16 [8, 4, 17, 256, 256], P(('groups', 'sec'), 'blk'), parts along dimension 0, may hold values from -0.375 to 0.375
- sources: int32 [8, 4, 17], P(('groups', 'sec'), 'blk'), parts along dimension 0, may hold values from 0 to 3, as said below
Outputs:
- applied: bfloat16 [8, 4, 256, 256], P(('groups', 'sec'), 'blk'), parts along dimension 0
- rayleigh: float32 [8], P(('groups', 'sec')), parts along dimension 0
- residual_scale: float32 [8], P(('groups', 'sec')), parts along dimension 0
The draws below stay inside these ranges and needn't reach their ends.
There are 2 independent parts, one for each index of `groups`. The reference program is written for one: setup_inputs(seed, part) draws one part's arguments, and reference() takes and returns one part's arrays. A program takes and returns all parts, laid end to end along the dimension named above; each array names one. Nothing has to cross between parts.
Inputs may be any that keep to these rules, and one draw needn't show every extreme that they name: `sources`: every entry names a sector of the same section, and the 17 channels of each output sector name every one of the 4 sectors of its section.
All inputs are finite; a program needn't handle non-finite values.
Results may differ from the reference program's by a relative error of at most 0.0064.
Values may be sent and summed in bfloat16 or wider, within the bound.
A program may use at most 64 MiB of HBM per device.

```python
import jax
import jax.numpy as jnp
from jax import lax

SB = 256
CH = 17
SEC_DEV = 1
SECTORS = 4
NSECT = 4


def draw_sources(key, part):
    blocks = SECTORS // SEC_DEV
    pairs = SEC_DEV * CH
    keys = jax.random.split(jax.random.fold_in(key, 11), NSECT * blocks)

    def single(subkey):
        first_key, second_key = jax.random.split(subkey)
        order = jax.random.permutation(first_key, blocks)
        offset = jax.random.randint(second_key, (), 0, SEC_DEV)
        slots = jnp.arange(pairs)
        device = order[slots % blocks]
        local = (slots // blocks + offset) % SEC_DEV
        return device * SEC_DEV + local
    table = jax.vmap(single)(keys)
    return table.reshape(NSECT, SECTORS, CH).astype(jnp.int32)


def levels(stream_key, dims, pieces, least, largest):
    gain = 1.0
    for dim, blocks in pieces:
        draws = jax.random.uniform(jax.random.fold_in(jax.random.fold_in(stream_key, 6), dim), (blocks,), jnp.float32, least / len(pieces), largest / len(pieces))
        gain = gain * jnp.repeat(jnp.exp(draws), dims[dim] // blocks).reshape((-1,) + (1,) * (len(dims) - 1 - dim))
    return gain


def centred(own_key, dims, deviation, most, pieces=(), kind=jnp.bfloat16):
    entries = deviation * jax.random.normal(own_key, dims, jnp.float32)
    if pieces:
        entries = entries * levels(own_key, dims, pieces, -0.22, 0.18)
    return jnp.clip(entries, -most, most).astype(kind)


def setup_inputs(seed: int = 0, part: int = 0) -> dict:
    key_list = jax.random.split(jax.random.key(seed), 5)
    own_keys = jax.random.split(jax.random.fold_in(key_list[4], part), 5)
    return {
        "psi": centred(own_keys[0], (NSECT, SECTORS, SB, SB), 1.0, 6.0, ((0, 4), (1, 4))),
        "own_env": centred(own_keys[1], (NSECT, SECTORS, CH, SB, SB), SB ** -0.5, 0.375, ((0, 4), (1, 4))),
        "handoff_env": centred(own_keys[2], (NSECT, SECTORS, CH, SB, SB), SB ** -0.5, 0.375, ((0, 4), (1, 4))),
        "sources": draw_sources(jax.random.fold_in(jax.random.fold_in(key_list[4], part), 71), part),
    }


def contract(picked, left, right):
    inner = jnp.einsum('qcab,qcbd->qcad', picked.astype(jnp.float32), right.astype(jnp.float32)).astype(jnp.bfloat16)
    return jnp.einsum('qcab,qcbd->qad', left.astype(jnp.float32), inner.astype(jnp.float32))

def section_step(item):
    vector, own, other, source, even = item
    left = jnp.where(even, own, other)
    right = jnp.where(even, other, own)
    first = contract(vector[source], left, right)
    widened = vector.astype(jnp.float32)
    along = jnp.sum(widened * first)
    mass = jnp.sum(widened * widened)
    alpha = along / mass
    resid = first - alpha * widened
    scale = jnp.sqrt(jnp.mean(resid * resid) + 1e-06)
    second = (resid / scale).astype(jnp.bfloat16)
    applied = contract(second[source], left, right).astype(jnp.bfloat16)
    return (applied, alpha, scale)

def reference(psi, own_env, handoff_env, sources):
    partner = handoff_env[jnp.arange(NSECT, dtype=jnp.int32) ^ 1]
    even = jnp.arange(NSECT, dtype=jnp.int32) % 2 == 0
    applied, alpha, scale = lax.map(section_step, (psi, own_env, partner, sources, even))
    return (applied, alpha, scale)
```

```python
import functools

import jax
import jax.numpy as jnp
from jax import lax
from jax.experimental import pallas as pl
from jax.experimental.pallas import tpu as pltpu
from jax.sharding import PartitionSpec as P

MESH = pl.DeviceIdType.MESH


def kernel(
    width, pieces,
    psi_hbm, own_hbm, hand_hbm, src_ref,
    out_ref, alpha_ref, scale_ref,
    env, whole, whole2, first_ref, stats,
    load_sem, z_send, z_recv, psi_send, psi_recv, stat_send, stat_recv,
    v_send, v_recv, f_send, f_recv,
):
    channels = own_hbm.shape[2]
    block = psi_hbm.shape[2]
    sec = lax.axis_index("sec")
    me = lax.axis_index("blk")
    odd = lax.rem(sec, 2)
    partner = {"sec": sec + 1 - 2 * odd}
    core = lax.rem(me, 2)
    sibling = me + 1 - 2 * core
    peers = [lax.rem(me + k, width) for k in range(1, width)]
    across = [lax.rem(me + 2 * k, width) for k in range(1, width // 2)]
    behind = [lax.rem(me + width - 2 * k, width) for k in range(1, width // 2)]
    sib_behind = [lax.rem(sibling + width - 2 * k, width) for k in range(1, width // 2)]

    barrier = pltpu.get_barrier_semaphore()
    pl.semaphore_signal(barrier, inc=1, device_id=partner, device_id_type=MESH)
    for k in peers:
        pl.semaphore_signal(barrier, inc=1, device_id={"blk": k}, device_id_type=MESH)
    load_own = pltpu.make_async_copy(own_hbm.at[0, 0], env.at[0], load_sem.at[0])
    load_psi = pltpu.make_async_copy(psi_hbm.at[0, 0], whole.at[me], load_sem.at[1])
    load_own.start()
    load_psi.start()
    pl.semaphore_wait(barrier, width)

    def z_copy(c):
        return pltpu.make_async_remote_copy(
            src_ref=hand_hbm.at[0, 0, c], dst_ref=env.at[1, c],
            send_sem=z_send.at[c], recv_sem=z_recv.at[c],
            device_id=partner, device_id_type=MESH,
        )

    @pl.loop(0, channels)
    def _(c):
        z_copy(c).start()

    def psi_copy(k):
        return pltpu.make_async_remote_copy(
            src_ref=psi_hbm.at[0, 0], dst_ref=whole.at[me],
            send_sem=psi_send.at[k], recv_sem=psi_recv.at[k],
            device_id={"blk": peers[k]}, device_id_type=MESH,
        )

    for k in range(width - 1):
        psi_copy(k).start()
    load_own.wait()
    load_psi.wait()
    for k in range(width - 1):
        psi_copy(k).wait()

    first_ref[...] = jnp.zeros_like(first_ref)

    def term(v, c):
        inner = jnp.dot(
            v[src_ref[0, 0, c]], env[1 - odd, c], preferred_element_type=jnp.float32
        ).astype(jnp.bfloat16)
        return jnp.dot(env[odd, c], inner, preferred_element_type=jnp.float32)

    @pl.loop(0, channels)
    def _(c):
        z_copy(c).wait_recv()
        first_ref[...] += term(whole, c)

    p = whole[me].astype(jnp.float32)
    f = first_ref[...]
    along = jnp.sum(p * f, keepdims=True)
    mass = jnp.sum(p * p, keepdims=True)
    own_alpha = jnp.where(mass > 0, along / jnp.where(mass > 0, mass, 1.0), 0.0)
    rest = f - own_alpha * p
    beside = jnp.sum(rest * rest, keepdims=True)
    row = lax.broadcasted_iota(jnp.int32, (8, 128), 0)
    stats[me] = jnp.where(row == 0, along, jnp.where(row == 1, mass, beside))

    def stat_copy(k):
        return pltpu.make_async_remote_copy(
            src_ref=stats.at[me], dst_ref=stats.at[me],
            send_sem=stat_send.at[k], recv_sem=stat_recv.at[k],
            device_id={"blk": peers[k]}, device_id_type=MESH,
        )

    for k in range(width - 1):
        stat_copy(k).start()
    for k in range(width - 1):
        stat_copy(k).wait()
    tiles = [stats[j] for j in range(width)]
    along_all = sum(t[0:1, 0:1] for t in tiles)
    mass_all = sum(t[1:2, 0:1] for t in tiles)
    alpha = along_all / mass_all
    power = jnp.zeros_like(alpha)
    for t in tiles:
        a, m, r = t[0:1, 0:1], t[1:2, 0:1], t[2:3, 0:1]
        off = jnp.where(m > 0, a / jnp.where(m > 0, m, 1.0), 0.0) - alpha
        power += r + off * off * m
    scale = jnp.sqrt(power / (width * block * block) + 1e-06)
    whole2[me] = ((f - alpha * p) / scale).astype(jnp.bfloat16)

    rows = block // pieces

    def v_copy(k, i):
        target = sibling if k < 0 else across[k]
        part = whole2.at[me, pl.ds(i * rows, rows)]
        return pltpu.make_async_remote_copy(
            src_ref=part, dst_ref=part,
            send_sem=v_send.at[k + 1, i], recv_sem=v_recv.at[k + 1, i],
            device_id={"blk": target}, device_id_type=MESH,
        )

    def f_copy(k, i):
        part = whole2.at[behind[k], pl.ds(i * rows, rows)]
        return pltpu.make_async_remote_copy(
            src_ref=part, dst_ref=part,
            send_sem=f_send.at[k, i], recv_sem=f_recv.at[k, i],
            device_id={"blk": sibling}, device_id_type=MESH,
        )

    hops = width // 2 - 1
    for k in range(hops):
        for i in range(pieces):
            v_copy(k, i).start()
    for i in range(pieces):
        v_copy(-1, i).start()
    for k in range(hops):
        for i in range(pieces):
            v_copy(k, i).wait_recv()
            f_copy(k, i).start()
    for i in range(pieces):
        v_copy(-1, i).wait_recv()
    for k in range(hops):
        for i in range(pieces):
            f_copy(k, i).wait_recv()

    total = term(whole2, 0)
    for c in range(1, channels):
        total += term(whole2, c)
    out_ref[0, 0] = total.astype(jnp.bfloat16)
    alpha_ref[0] = alpha[0, 0]
    scale_ref[0] = scale[0, 0]

    for k in range(-1, hops):
        for i in range(pieces):
            v_copy(k, i).wait_send()
    for k in range(hops):
        for i in range(pieces):
            f_copy(k, i).wait_send()

    @pl.loop(0, channels)
    def _(c):
        z_copy(c).wait_send()


def shards(width, psi, own_env, handoff_env, sources):
    channels = sources.shape[2]
    block = psi.shape[2]
    pieces = 2
    hops = width // 2 - 1
    dma = pltpu.SemaphoreType.DMA
    bf16, f32 = jnp.bfloat16, jnp.float32
    hbm = pl.BlockSpec(memory_space=pl.ANY)
    return pl.pallas_call(
        functools.partial(kernel, width, pieces),
        out_shape=(
            jax.ShapeDtypeStruct(psi.shape, bf16),
            jax.ShapeDtypeStruct((1,), f32),
            jax.ShapeDtypeStruct((1,), f32),
        ),
        in_specs=[hbm, hbm, hbm, pl.BlockSpec(memory_space=pltpu.SMEM)],
        out_specs=(
            pl.BlockSpec(memory_space=pltpu.VMEM),
            pl.BlockSpec(memory_space=pltpu.SMEM),
            pl.BlockSpec(memory_space=pltpu.SMEM),
        ),
        scratch_shapes=[
            pltpu.VMEM((2, channels, block, block), bf16),
            pltpu.VMEM((width, block, block), bf16),
            pltpu.VMEM((width, block, block), bf16),
            pltpu.VMEM((block, block), f32),
            pltpu.VMEM((width, 8, 128), f32),
            dma((2,)),
            dma((channels,)), dma((channels,)),
            dma((width - 1,)), dma((width - 1,)),
            dma((width - 1,)), dma((width - 1,)),
            dma((hops + 1, pieces)), dma((hops + 1, pieces)),
            dma((hops, pieces)), dma((hops, pieces)),
        ],
        compiler_params=pltpu.CompilerParams(
            collective_id=0, has_side_effects=True, vmem_limit_bytes=40 * 2**20
        ),
        cost_estimate=pl.CostEstimate(
            flops=8 * channels * block**3, bytes_accessed=6 * channels * block**2,
            transcendentals=0,
        ),
    )(psi, own_env, handoff_env, sources)


def solution(mesh):
    in_specs = (
        P(("groups", "sec"), "blk", None, None),
        P(("groups", "sec"), "blk", None, None, None),
        P(("groups", "sec"), "blk", None, None, None),
        P(("groups", "sec"), "blk", None),
    )
    out_specs = (
        P(("groups", "sec"), "blk", None, None),
        P(("groups", "sec")),
        P(("groups", "sec")),
    )
    body = functools.partial(shards, mesh.shape["blk"])
    return jax.shard_map(body, mesh=mesh, in_specs=in_specs, out_specs=out_specs, check_vma=False)
```

```python
import functools

import jax
import jax.numpy as jnp
from jax import lax
from jax.experimental import pallas as pl
from jax.experimental.pallas import tpu as pltpu
from jax.sharding import PartitionSpec as P

MESH = pl.DeviceIdType.MESH


def kernel(
    width, pieces,
    psi_hbm, own_hbm, hand_hbm, src_ref,
    out_ref, alpha_ref, scale_ref,
    env, whole, whole2, first_ref, part_ref, tail_ref, full_ref,
    load_sem, z_send, z_recv, psi_send, psi_recv, *relay_sems,
):
    early_sems, late_sems = relay_sems[:4], relay_sems[4:]
    channels = own_hbm.shape[2]
    block = psi_hbm.shape[2]
    sec = lax.axis_index("sec")
    me = lax.axis_index("blk")
    odd = lax.rem(sec, 2)
    partner = {"sec": sec + 1 - 2 * odd}
    core = lax.rem(me, 2)
    sibling = me + 1 - 2 * core
    peers = [lax.rem(me + k, width) for k in range(1, width)]
    across = [lax.rem(me + 2 * k, width) for k in range(1, width // 2)]
    behind = [lax.rem(me + width - 2 * k, width) for k in range(1, width // 2)]
    sib_behind = [lax.rem(sibling + width - 2 * k, width) for k in range(1, width // 2)]

    barrier = pltpu.get_barrier_semaphore()
    pl.semaphore_signal(barrier, inc=1, device_id=partner, device_id_type=MESH)
    for k in peers:
        pl.semaphore_signal(barrier, inc=1, device_id={"blk": k}, device_id_type=MESH)
    load_own = pltpu.make_async_copy(own_hbm.at[0, 0], env.at[0], load_sem.at[0])
    load_psi = pltpu.make_async_copy(psi_hbm.at[0, 0], whole.at[me], load_sem.at[1])
    load_own.start()
    load_psi.start()
    pl.semaphore_wait(barrier, width)

    def z_copy(c):
        return pltpu.make_async_remote_copy(
            src_ref=hand_hbm.at[0, 0, c], dst_ref=env.at[1, c],
            send_sem=z_send.at[c], recv_sem=z_recv.at[c],
            device_id=partner, device_id_type=MESH,
        )

    @pl.loop(0, channels)
    def _(c):
        z_copy(c).start()

    def psi_copy(k):
        return pltpu.make_async_remote_copy(
            src_ref=psi_hbm.at[0, 0], dst_ref=whole.at[me],
            send_sem=psi_send.at[k], recv_sem=psi_recv.at[k],
            device_id={"blk": peers[k]}, device_id_type=MESH,
        )

    for k in range(width - 1):
        psi_copy(k).start()
    load_own.wait()
    load_psi.wait()
    for k in range(width - 1):
        psi_copy(k).wait()

    def term(v, c):
        inner = jnp.dot(
            v[src_ref[0, 0, c]], env[1 - odd, c], preferred_element_type=jnp.float32
        ).astype(jnp.bfloat16)
        return jnp.dot(env[odd, c], inner, preferred_element_type=jnp.float32)

    rows = block // pieces
    hops = width // 2 - 1

    def relay(buf, sems):
        v_send, v_recv, f_send, f_recv = sems

        def direct(k, i):
            part = buf.at[me, pl.ds(i * rows, rows)]
            return pltpu.make_async_remote_copy(
                src_ref=part, dst_ref=part,
                send_sem=v_send.at[k + 1, i], recv_sem=v_recv.at[k + 1, i],
                device_id={"blk": sibling if k < 0 else across[k]}, device_id_type=MESH,
            )

        def passed(k, i):
            part = buf.at[behind[k], pl.ds(i * rows, rows)]
            return pltpu.make_async_remote_copy(
                src_ref=part, dst_ref=part,
                send_sem=f_send.at[k, i], recv_sem=f_recv.at[k, i],
                device_id={"blk": sibling}, device_id_type=MESH,
            )

        def start():
            for k in [*range(hops), -1]:
                for i in range(pieces):
                    direct(k, i).start()

        def forward():
            for k in range(hops):
                for i in range(pieces):
                    direct(k, i).wait_recv()
                    passed(k, i).start()

        def arrive():
            for i in range(pieces):
                direct(-1, i).wait_recv()
            for k in range(hops):
                for i in range(pieces):
                    passed(k, i).wait_recv()

        def drain():
            for i in range(pieces):
                for k in range(-1, hops):
                    direct(k, i).wait_send()
                for k in range(hops):
                    passed(k, i).wait_send()

        return start, forward, arrive, drain

    early = relay(part_ref, early_sems)
    late = relay(tail_ref, late_sems)

    def channels_from(lo, hi):
        first_ref[...] = jnp.zeros_like(first_ref)
        add_channels(lo, hi)

    def add_channels(lo, hi):
        @pl.loop(lo, hi)
        def _(c):
            z_copy(c).wait_recv()
            first_ref[...] += term(whole, c)

    cut = max(channels - 5, 0)
    channels_from(0, cut)
    part_ref[me] = first_ref[...]
    early[0]()
    channels_from(cut, cut + 3)
    early[1]()
    add_channels(cut + 3, channels - 1)
    early[2]()

    def fold(x):
        return jnp.sum(x.reshape(block // 8, 8, block), axis=0)

    mass = jnp.zeros((8, block), jnp.float32)
    for j in range(width):
        p = whole[j].astype(jnp.float32)
        mass += fold(p * p)
    mass = jnp.sum(mass, keepdims=True)
    add_channels(channels - 1, channels)
    tail_ref[me] = first_ref[...].astype(jnp.bfloat16)
    late[0]()
    early[3]()
    late[1]()
    late[2]()

    along = jnp.zeros((8, block), jnp.float32)
    for j in range(width):
        f = part_ref[j] + tail_ref[j].astype(jnp.float32)
        full_ref[j] = f
        along += fold(whole[j].astype(jnp.float32) * f)
    alpha = jnp.sum(along, keepdims=True) / mass
    power = jnp.zeros((8, block), jnp.float32)
    for j in range(width):
        rest = full_ref[j] - alpha * whole[j].astype(jnp.float32)
        full_ref[j] = rest
        power += fold(rest * rest)
    scale = jnp.sqrt(jnp.sum(power, keepdims=True) / (width * block * block) + 1e-06)
    factor = 1.0 / scale
    for j in range(width):
        whole2[j] = (full_ref[j] * factor).astype(jnp.bfloat16)

    total = term(whole2, 0)
    for c in range(1, channels):
        total += term(whole2, c)
    out_ref[0, 0] = total.astype(jnp.bfloat16)
    alpha_ref[0] = alpha[0, 0]
    scale_ref[0] = scale[0, 0]

    late[3]()

    @pl.loop(0, channels)
    def _(c):
        z_copy(c).wait_send()


def shards(width, psi, own_env, handoff_env, sources):
    channels = sources.shape[2]
    block = psi.shape[2]
    pieces = 2
    hops = width // 2 - 1
    dma = pltpu.SemaphoreType.DMA
    bf16, f32 = jnp.bfloat16, jnp.float32
    hbm = pl.BlockSpec(memory_space=pltpu.HBM)
    return pl.pallas_call(
        functools.partial(kernel, width, pieces),
        out_shape=(
            jax.ShapeDtypeStruct(psi.shape, bf16),
            jax.ShapeDtypeStruct((1,), f32),
            jax.ShapeDtypeStruct((1,), f32),
        ),
        in_specs=[hbm, hbm, hbm, pl.BlockSpec(memory_space=pltpu.SMEM)],
        out_specs=(
            pl.BlockSpec(memory_space=pltpu.VMEM),
            pl.BlockSpec(memory_space=pltpu.SMEM),
            pl.BlockSpec(memory_space=pltpu.SMEM),
        ),
        scratch_shapes=[
            pltpu.VMEM((2, channels, block, block), bf16),
            pltpu.VMEM((width, block, block), bf16),
            pltpu.VMEM((width, block, block), bf16),
            pltpu.VMEM((block, block), f32),
            pltpu.VMEM((width, block, block), f32),
            pltpu.VMEM((width, block, block), bf16),
            pltpu.VMEM((width, block, block), f32),
            dma((2,)),
            dma((channels,)), dma((channels,)),
            dma((width - 1,)), dma((width - 1,)),
            *[dma((n, pieces)) for n in (hops + 1, hops + 1, hops, hops) * 2],
        ],
        compiler_params=pltpu.CompilerParams(
            collective_id=0, has_side_effects=True, vmem_limit_bytes=62 * 2**20
        ),
        cost_estimate=pl.CostEstimate(
            flops=8 * channels * block**3, bytes_accessed=6 * channels * block**2,
            transcendentals=0,
        ),
    )(psi, own_env, handoff_env, sources)


def solution(mesh):
    in_specs = (
        P(("groups", "sec"), "blk", None, None),
        P(("groups", "sec"), "blk", None, None, None),
        P(("groups", "sec"), "blk", None, None, None),
        P(("groups", "sec"), "blk", None),
    )
    out_specs = (
        P(("groups", "sec"), "blk", None, None),
        P(("groups", "sec")),
        P(("groups", "sec")),
    )
    body = functools.partial(shards, mesh.shape["blk"])
    return jax.shard_map(body, mesh=mesh, in_specs=in_specs, out_specs=out_specs, check_vma=False)
```

```python
import functools

import jax
import jax.numpy as jnp
from jax import lax
from jax.experimental import pallas as pl
from jax.experimental.pallas import tpu as pltpu
from jax.sharding import PartitionSpec as P

MESH = pl.DeviceIdType.MESH


def kernel(
    width,
    psi_hbm, own_hbm, hand_hbm, src_ref,
    out_ref, alpha_ref, scale_ref,
    env, whole, whole2, first_ref, part_ref, tail_ref, psi_ref,
    load_sem, z_send, z_recv, psi_send, psi_recv, *relay_sems,
):
    channels = own_hbm.shape[2]
    block = psi_hbm.shape[2]
    half = block // 2
    sec = lax.axis_index("sec")
    me = lax.axis_index("blk")
    odd = lax.rem(sec, 2)
    partner = {"sec": sec + 1 - 2 * odd}
    core = lax.rem(me, 2)
    sibling = me + 1 - 2 * core
    peers = [lax.rem(me + k, width) for k in range(1, width)]
    across = [lax.rem(me + 2 * k, width) for k in range(1, width // 2)]
    behind = [lax.rem(me + width - 2 * k, width) for k in range(1, width // 2)]
    sib_behind = [lax.rem(sibling + width - 2 * k, width) for k in range(1, width // 2)]

    barrier = pltpu.get_barrier_semaphore()
    pl.semaphore_signal(barrier, inc=1, device_id=partner, device_id_type=MESH)
    for k in peers:
        pl.semaphore_signal(barrier, inc=1, device_id={"blk": k}, device_id_type=MESH)
    load_own = pltpu.make_async_copy(own_hbm.at[0, 0], env.at[0], load_sem.at[0])
    load_psi = pltpu.make_async_copy(psi_hbm.at[0, 0], whole.at[me], load_sem.at[1])
    load_own.start()
    load_psi.start()
    pl.semaphore_wait(barrier, width)

    def z_copy(by_rows, h, c):
        cut = (pl.ds(h * half, half), slice(None))
        cut = cut if by_rows else cut[::-1]
        return pltpu.make_async_remote_copy(
            src_ref=hand_hbm.at[(0, 0, c, *cut)], dst_ref=env.at[(1, c, *cut)],
            send_sem=z_send.at[h, c], recv_sem=z_recv.at[h, c],
            device_id=partner, device_id_type=MESH,
        )

    def outgoing(act):
        for parity in range(2):
            @pl.when(odd == parity)
            def _():
                for h in range(2):
                    @pl.loop(0, channels)
                    def _(c):
                        act(z_copy(parity == 0, h, c))

    outgoing(lambda copy: copy.start())

    def psi_copy(k):
        return pltpu.make_async_remote_copy(
            src_ref=psi_hbm.at[0, 0], dst_ref=whole.at[me],
            send_sem=psi_send.at[k], recv_sem=psi_recv.at[k],
            device_id={"blk": peers[k]}, device_id_type=MESH,
        )

    for k in range(width - 1):
        psi_copy(k).start()
    load_own.wait()
    load_psi.wait()
    for k in range(width - 1):
        psi_copy(k).wait()

    def term(v, c):
        inner = jnp.dot(
            v[src_ref[0, 0, c]], env[1 - odd, c], preferred_element_type=jnp.float32
        ).astype(jnp.bfloat16)
        return jnp.dot(env[odd, c], inner, preferred_element_type=jnp.float32)

    pieces = 2
    hops = width // 2 - 1

    def relay(buf, lo, sems):
        v_send, v_recv, f_send, f_recv = sems

        def direct(k, i):
            part = buf.at[me, lo + i]
            return pltpu.make_async_remote_copy(
                src_ref=part, dst_ref=part,
                send_sem=v_send.at[k + 1, i], recv_sem=v_recv.at[k + 1, i],
                device_id={"blk": sibling if k < 0 else across[k]}, device_id_type=MESH,
            )

        def passed(k, i):
            part = buf.at[behind[k], lo + i]
            return pltpu.make_async_remote_copy(
                src_ref=part, dst_ref=part,
                send_sem=f_send.at[k, i], recv_sem=f_recv.at[k, i],
                device_id={"blk": sibling}, device_id_type=MESH,
            )

        def start():
            for k in [*range(hops), -1]:
                for i in range(pieces):
                    direct(k, i).start()

        def forward():
            for k in range(hops):
                for i in range(pieces):
                    direct(k, i).wait_recv()
                    passed(k, i).start()

        def arrive():
            for i in range(pieces):
                direct(-1, i).wait_recv()
            for k in range(hops):
                for i in range(pieces):
                    passed(k, i).wait_recv()

        def drain():
            for i in range(pieces):
                for k in range(-1, hops):
                    direct(k, i).wait_send()
                for k in range(hops):
                    passed(k, i).wait_send()

        return start, forward, arrive, drain

    upper, lower = 2 - odd, 1 + odd
    head = relay(part_ref, 0, relay_sems[:4])
    early = relay(part_ref, 2, relay_sems[4:8])
    late = relay(tail_ref, 0, relay_sems[8:])

    def add_channels(h, lo, hi):
        cut = pl.ds(h * half, half)

        @pl.when(odd == 0)
        def _():
            @pl.loop(lo, hi)
            def _(c):
                z_copy(False, h, c).wait_recv()
                inner = jnp.dot(
                    whole[src_ref[0, 0, c]], env[1, c, :, cut], preferred_element_type=jnp.float32
                ).astype(jnp.bfloat16)
                x = jnp.dot(env[0, c], inner, preferred_element_type=jnp.float32)
                first_ref[0] += x[:half]
                first_ref[1] += x[half:]

        @pl.when(odd == 1)
        def _():
            @pl.loop(lo, hi)
            def _(c):
                z_copy(True, h, c).wait_recv()
                inner = jnp.dot(
                    whole[src_ref[0, 0, c]], env[0, c], preferred_element_type=jnp.float32
                ).astype(jnp.bfloat16)
                x = jnp.dot(env[1, c, cut, :], inner, preferred_element_type=jnp.float32)
                first_ref[0] += x[:, :half]
                first_ref[1] += x[:, half:]

    def fold(x):
        return jnp.sum(x.reshape(-1, 8, half), axis=0)

    cut = max(channels - 6, 0)
    first_ref[...] = jnp.zeros_like(first_ref)
    add_channels(0, 0, channels)
    part_ref[me, 0:2] = first_ref[...]
    head[0]()
    first_ref[...] = jnp.zeros_like(first_ref)
    mass = jnp.zeros((8, half), jnp.float32)
    for j in range(width):
        p = whole[j]
        psi_ref[j, 0] = p[:half, :half]
        psi_ref[j, 3] = p[half:, half:]
        psi_ref[j, upper] = p[:half, half:]
        psi_ref[j, lower] = p[half:, :half]
        p = psi_ref[j].astype(jnp.float32)
        mass += fold(p * p)
    mass = jnp.sum(mass, keepdims=True)
    add_channels(1, 0, cut // 2)
    head[1]()
    add_channels(1, cut // 2, cut)
    part_ref[me, 2:4] = first_ref[...]
    first_ref[...] = jnp.zeros_like(first_ref)
    early[0]()
    head[2]()
    head[3]()
    add_channels(1, cut, channels - 3)
    early[1]()
    add_channels(1, channels - 3, channels - 1)
    early[2]()
    early[3]()
    add_channels(1, channels - 1, channels)
    tail_ref[me] = first_ref[...].astype(jnp.bfloat16)
    late[0]()
    late[1]()
    late[2]()

    along = jnp.zeros((8, half), jnp.float32)
    for j in range(width):
        part_ref[j, 2:4] += tail_ref[j].astype(jnp.float32)
        along += fold(psi_ref[j].astype(jnp.float32) * part_ref[j])
    alpha = jnp.sum(along, keepdims=True) / mass
    power = jnp.zeros((8, half), jnp.float32)
    for j in range(width):
        rest = part_ref[j] - alpha * psi_ref[j].astype(jnp.float32)
        part_ref[j] = rest
        power += fold(rest * rest)
    scale = jnp.sqrt(jnp.sum(power, keepdims=True) / (width * block * block) + 1e-06)
    factor = 1.0 / scale
    for j in range(width):
        whole2[j, :half, :half] = (part_ref[j, 0] * factor).astype(jnp.bfloat16)
        whole2[j, :half, half:] = (part_ref[j, upper] * factor).astype(jnp.bfloat16)
        whole2[j, half:, :half] = (part_ref[j, lower] * factor).astype(jnp.bfloat16)
        whole2[j, half:, half:] = (part_ref[j, 3] * factor).astype(jnp.bfloat16)

    total = term(whole2, 0)
    for c in range(1, channels):
        total += term(whole2, c)
    out_ref[0, 0] = total.astype(jnp.bfloat16)
    alpha_ref[0] = alpha[0, 0]
    scale_ref[0] = scale[0, 0]

    late[3]()

    outgoing(lambda copy: copy.wait_send())


def shards(width, psi, own_env, handoff_env, sources):
    channels = sources.shape[2]
    block = psi.shape[2]
    half = block // 2
    hops = width // 2 - 1
    dma = pltpu.SemaphoreType.DMA
    bf16, f32 = jnp.bfloat16, jnp.float32
    hbm = pl.BlockSpec(memory_space=pltpu.HBM)
    return pl.pallas_call(
        functools.partial(kernel, width),
        out_shape=(
            jax.ShapeDtypeStruct(psi.shape, bf16),
            jax.ShapeDtypeStruct((1,), f32),
            jax.ShapeDtypeStruct((1,), f32),
        ),
        in_specs=[hbm, hbm, hbm, pl.BlockSpec(memory_space=pltpu.SMEM)],
        out_specs=(
            pl.BlockSpec(memory_space=pltpu.VMEM),
            pl.BlockSpec(memory_space=pltpu.SMEM),
            pl.BlockSpec(memory_space=pltpu.SMEM),
        ),
        scratch_shapes=[
            pltpu.VMEM((2, channels, block, block), bf16),
            pltpu.VMEM((width, block, block), bf16),
            pltpu.VMEM((width, block, block), bf16),
            pltpu.VMEM((2, half, half), f32),
            pltpu.VMEM((width, 4, half, half), f32),
            pltpu.VMEM((width, 2, half, half), bf16),
            pltpu.VMEM((width, 4, half, half), bf16),
            dma((2,)),
            dma((2, channels)), dma((2, channels)),
            dma((width - 1,)), dma((width - 1,)),
            *[dma((n, 2)) for n in (hops + 1, hops + 1, hops, hops) * 3],
        ],
        compiler_params=pltpu.CompilerParams(
            collective_id=0, has_side_effects=True, vmem_limit_bytes=62 * 2**20
        ),
        cost_estimate=pl.CostEstimate(
            flops=8 * channels * block**3, bytes_accessed=6 * channels * block**2,
            transcendentals=0,
        ),
    )(psi, own_env, handoff_env, sources)


def solution(mesh):
    in_specs = (
        P(("groups", "sec"), "blk", None, None),
        P(("groups", "sec"), "blk", None, None, None),
        P(("groups", "sec"), "blk", None, None, None),
        P(("groups", "sec"), "blk", None),
    )
    out_specs = (
        P(("groups", "sec"), "blk", None, None),
        P(("groups", "sec")),
        P(("groups", "sec")),
    )
    body = functools.partial(shards, mesh.shape["blk"])
    return jax.shard_map(body, mesh=mesh, in_specs=in_specs, out_specs=out_specs, check_vma=False)
```

```python
import functools

import jax
import jax.numpy as jnp
from jax import lax
from jax.experimental import pallas as pl
from jax.experimental.pallas import tpu as pltpu
from jax.sharding import PartitionSpec as P

MESH = pl.DeviceIdType.MESH


def kernel(
    width,
    psi_hbm, own_hbm, hand_hbm, src_ref,
    out_ref, alpha_ref, scale_ref,
    env, whole, whole2, first_ref, part_ref, psi_ref, rest_ref,
    load_sem, z_send, z_recv, psi_send, psi_recv, *relay_sems,
):
    channels = own_hbm.shape[2]
    block = psi_hbm.shape[2]
    half = block // 2
    sec = lax.axis_index("sec")
    me = lax.axis_index("blk")
    odd = lax.rem(sec, 2)
    partner = {"sec": sec + 1 - 2 * odd}
    core = lax.rem(me, 2)
    sibling = me + 1 - 2 * core
    peers = [lax.rem(me + k, width) for k in range(1, width)]
    across = [lax.rem(me + 2 * k, width) for k in range(1, width // 2)]
    behind = [lax.rem(me + width - 2 * k, width) for k in range(1, width // 2)]
    sib_behind = [lax.rem(sibling + width - 2 * k, width) for k in range(1, width // 2)]

    barrier = pltpu.get_barrier_semaphore()
    pl.semaphore_signal(barrier, inc=1, device_id=partner, device_id_type=MESH)
    for k in peers:
        pl.semaphore_signal(barrier, inc=1, device_id={"blk": k}, device_id_type=MESH)
    load_own = pltpu.make_async_copy(own_hbm.at[0, 0], env.at[0], load_sem.at[0])
    load_psi = pltpu.make_async_copy(psi_hbm.at[0, 0], whole.at[me], load_sem.at[1])
    load_own.start()
    load_psi.start()
    pl.semaphore_wait(barrier, width)

    def z_copy(by_rows, h, c):
        cut = (pl.ds(h * half, half), slice(None))
        cut = cut if by_rows else cut[::-1]
        return pltpu.make_async_remote_copy(
            src_ref=hand_hbm.at[(0, 0, c, *cut)], dst_ref=env.at[(1, c, *cut)],
            send_sem=z_send.at[h, c], recv_sem=z_recv.at[h, c],
            device_id=partner, device_id_type=MESH,
        )

    def outgoing(act):
        for parity in range(2):
            @pl.when(odd == parity)
            def _():
                for h in range(2):
                    @pl.loop(0, channels)
                    def _(c):
                        act(z_copy(parity == 0, h, c))

    outgoing(lambda copy: copy.start())

    def psi_copy(k):
        return pltpu.make_async_remote_copy(
            src_ref=psi_hbm.at[0, 0], dst_ref=whole.at[me],
            send_sem=psi_send.at[k], recv_sem=psi_recv.at[k],
            device_id={"blk": peers[k]}, device_id_type=MESH,
        )

    for k in range(width - 1):
        psi_copy(k).start()
    load_own.wait()
    load_psi.wait()
    for k in range(width - 1):
        psi_copy(k).wait()

    def term(v, c):
        inner = jnp.dot(
            v[src_ref[0, 0, c]], env[1 - odd, c], preferred_element_type=jnp.float32
        ).astype(jnp.bfloat16)
        return jnp.dot(env[odd, c], inner, preferred_element_type=jnp.float32)

    pieces = 2
    hops = width // 2 - 1

    def relay(buf, lo, sems):
        v_send, v_recv, f_send, f_recv = sems

        def direct(k, i):
            part = buf.at[me, lo + i]
            return pltpu.make_async_remote_copy(
                src_ref=part, dst_ref=part,
                send_sem=v_send.at[k + 1, i], recv_sem=v_recv.at[k + 1, i],
                device_id={"blk": sibling if k < 0 else across[k]}, device_id_type=MESH,
            )

        def passed(k, i):
            part = buf.at[behind[k], lo + i]
            return pltpu.make_async_remote_copy(
                src_ref=part, dst_ref=part,
                send_sem=f_send.at[k, i], recv_sem=f_recv.at[k, i],
                device_id={"blk": sibling}, device_id_type=MESH,
            )

        def start():
            for k in [*range(hops), -1]:
                for i in range(pieces):
                    direct(k, i).start()

        def forward():
            for k in range(hops):
                for i in range(pieces):
                    direct(k, i).wait_recv()
                    passed(k, i).start()

        def arrive():
            for i in range(pieces):
                direct(-1, i).wait_recv()
            for k in range(hops):
                for i in range(pieces):
                    passed(k, i).wait_recv()

        def drain():
            for i in range(pieces):
                for k in range(-1, hops):
                    direct(k, i).wait_send()
                for k in range(hops):
                    passed(k, i).wait_send()

        return start, forward, arrive, drain

    upper, lower = 2 - odd, 1 + odd
    head = relay(part_ref, 0, relay_sems[:4])
    late = relay(part_ref, 2, relay_sems[4:])

    def add_channels(h, lo, hi):
        cut = pl.ds(h * half, half)

        @pl.when(odd == 0)
        def _():
            @pl.loop(lo, hi)
            def _(c):
                z_copy(False, h, c).wait_recv()
                inner = jnp.dot(
                    whole[src_ref[0, 0, c]], env[1, c, :, cut], preferred_element_type=jnp.float32
                ).astype(jnp.bfloat16)
                x = jnp.dot(env[0, c], inner, preferred_element_type=jnp.float32)
                first_ref[0] += x[:half]
                first_ref[1] += x[half:]

        @pl.when(odd == 1)
        def _():
            @pl.loop(lo, hi)
            def _(c):
                z_copy(True, h, c).wait_recv()
                inner = jnp.dot(
                    whole[src_ref[0, 0, c]], env[0, c], preferred_element_type=jnp.float32
                ).astype(jnp.bfloat16)
                x = jnp.dot(env[1, c, cut, :], inner, preferred_element_type=jnp.float32)
                first_ref[0] += x[:, :half]
                first_ref[1] += x[:, half:]

    def fold(x):
        return jnp.sum(x.reshape(-1, 8, half), axis=0)

    cut = max(channels - 6, 0)
    first_ref[...] = jnp.zeros_like(first_ref)
    add_channels(0, 0, channels)
    part_ref[me, 0:2] = first_ref[...]
    head[0]()
    first_ref[...] = jnp.zeros_like(first_ref)
    mass = jnp.zeros((8, half), jnp.float32)
    for j in range(width):
        p = whole[j]
        psi_ref[j, 0] = p[:half, :half]
        psi_ref[j, 3] = p[half:, half:]
        psi_ref[j, upper] = p[:half, half:]
        psi_ref[j, lower] = p[half:, :half]
        p = psi_ref[j].astype(jnp.float32)
        mass += fold(p * p)
    mass = jnp.sum(mass, keepdims=True)
    add_channels(1, 0, cut // 2)
    head[1]()
    add_channels(1, cut // 2, cut)
    head[2]()
    head[3]()
    add_channels(1, cut, channels - 1)
    add_channels(1, channels - 1, channels)
    part_ref[me, 2:4] = first_ref[...]
    late[0]()
    late[1]()
    late[2]()

    along = jnp.zeros((8, half), jnp.float32)
    for j in range(width):
        along += fold(psi_ref[j].astype(jnp.float32) * part_ref[j])
    alpha = jnp.sum(along, keepdims=True) / mass
    power = jnp.zeros((8, half), jnp.float32)
    for j in range(width):
        rest = part_ref[j] - alpha * psi_ref[j].astype(jnp.float32)
        rest_ref[j] = rest
        power += fold(rest * rest)
    scale = jnp.sqrt(jnp.sum(power, keepdims=True) / (width * block * block) + 1e-06)
    factor = 1.0 / scale
    for j in range(width):
        whole2[j, :half, :half] = (rest_ref[j, 0] * factor).astype(jnp.bfloat16)
        whole2[j, :half, half:] = (rest_ref[j, upper] * factor).astype(jnp.bfloat16)
        whole2[j, half:, :half] = (rest_ref[j, lower] * factor).astype(jnp.bfloat16)
        whole2[j, half:, half:] = (rest_ref[j, 3] * factor).astype(jnp.bfloat16)

    total = term(whole2, 0)
    for c in range(1, channels):
        total += term(whole2, c)
    out_ref[0, 0] = total.astype(jnp.bfloat16)
    alpha_ref[0] = alpha[0, 0]
    scale_ref[0] = scale[0, 0]

    late[3]()

    outgoing(lambda copy: copy.wait_send())


def shards(width, psi, own_env, handoff_env, sources):
    channels = sources.shape[2]
    block = psi.shape[2]
    half = block // 2
    hops = width // 2 - 1
    dma = pltpu.SemaphoreType.DMA
    bf16, f32 = jnp.bfloat16, jnp.float32
    hbm = pl.BlockSpec(memory_space=pltpu.HBM)
    return pl.pallas_call(
        functools.partial(kernel, width),
        out_shape=(
            jax.ShapeDtypeStruct(psi.shape, bf16),
            jax.ShapeDtypeStruct((1,), f32),
            jax.ShapeDtypeStruct((1,), f32),
        ),
        in_specs=[hbm, hbm, hbm, pl.BlockSpec(memory_space=pltpu.SMEM)],
        out_specs=(
            pl.BlockSpec(memory_space=pltpu.VMEM),
            pl.BlockSpec(memory_space=pltpu.SMEM),
            pl.BlockSpec(memory_space=pltpu.SMEM),
        ),
        scratch_shapes=[
            pltpu.VMEM((2, channels, block, block), bf16),
            pltpu.VMEM((width, block, block), bf16),
            pltpu.VMEM((width, block, block), bf16),
            pltpu.VMEM((2, half, half), f32),
            pltpu.VMEM((width, 4, half, half), f32),
            pltpu.VMEM((width, 4, half, half), bf16),
            pltpu.VMEM((width, 4, half, half), f32),
            dma((2,)),
            dma((2, channels)), dma((2, channels)),
            dma((width - 1,)), dma((width - 1,)),
            *[dma((n, 2)) for n in (hops + 1, hops + 1, hops, hops) * 2],
        ],
        compiler_params=pltpu.CompilerParams(
            collective_id=0, has_side_effects=True, vmem_limit_bytes=62 * 2**20
        ),
        cost_estimate=pl.CostEstimate(
            flops=8 * channels * block**3, bytes_accessed=6 * channels * block**2,
            transcendentals=0,
        ),
    )(psi, own_env, handoff_env, sources)


def solution(mesh):
    in_specs = (
        P(("groups", "sec"), "blk", None, None),
        P(("groups", "sec"), "blk", None, None, None),
        P(("groups", "sec"), "blk", None, None, None),
        P(("groups", "sec"), "blk", None),
    )
    out_specs = (
        P(("groups", "sec"), "blk", None, None),
        P(("groups", "sec")),
        P(("groups", "sec")),
    )
    body = functools.partial(shards, mesh.shape["blk"])
    return jax.shard_map(body, mesh=mesh, in_specs=in_specs, out_specs=out_specs, check_vma=False)
```
